32 devices in a mesh: slide: 2 (over x), gr: 4 (over y, core), gc: 4 (over z).
Axes of the slice: x: 2, y: 2, z: 4, core: 2. Of those that a mesh axis runs over, the one named last changes fastest.
Arguments:
- features: bfloat16 [128, 32, 512], P(('slide', 'gr'), 'gc'), parts along dimension 0, may hold values from -6 to 6
- out_grad: bfloat16 [128, 32, 512], P(('slide', 'gr'), 'gc'), parts along dimension 0, may hold values from -6 to 6
- w_in: bfloat16 [512, 1024], replicated, may hold values from -0.25 to 0.25
- w_out: bfloat16 [1024, 512], replicated, may hold values from -0.1875 to 0.1875
- decay_row: bfloat16 [128, 32, 1024], P(('slide', 'gr'), 'gc'), parts along dimension 0, may hold values from 0 to 1, as said below
- decay_col: bfloat16 [128, 32, 1024], P(('slide', 'gr'), 'gc'), parts along dimension 0, may hold values from 0 to 1, as said below
- b_proj: float32 [128, 32, 16], P(('slide', 'gr'), 'gc'), parts along dimension 0, may hold values from -6 to 6
- c_proj: float32 [128, 32, 16], P(('slide', 'gr'), 'gc'), parts along dimension 0, may hold values from -6 to 6
- tissue: int32 [128, 32], P(('slide', 'gr'), 'gc'), parts along dimension 0, may hold values from 0 to 1, as said below
Outputs:
- feat_grad: bfloat16 [128, 32, 512], P(('slide', 'gr'), 'gc'), parts along dimension 0
- w_in_grad: float32 [1024, 1024], P('slide'), parts along dimension 0
- w_out_grad: float32 [2048, 512], P('slide'), parts along dimension 0
- decay_row_grad: float32 [128, 32, 1024], P(('slide', 'gr'), 'gc'), parts along dimension 0
- decay_col_grad: float32 [128, 32, 1024], P(('slide', 'gr'), 'gc'), parts along dimension 0
- b_grad: float32 [128, 32, 16], P(('slide', 'gr'), 'gc'), parts along dimension 0
- c_grad: float32 [128, 32, 16], P(('slide', 'gr'), 'gc'), parts along dimension 0
The draws below stay inside these ranges and needn't reach their ends.
There are 2 independent parts, one for each index of `slide`. The reference program is written for one: setup_inputs(seed, part) draws one part's arguments, and reference() takes and returns one part's arrays. A program takes and returns all parts, laid end to end along the dimension named above; an argument that names none is the same for every part. Nothing has to cross between parts.
Inputs may be any that keep to these rules, and one draw needn't show every extreme that they name: 1 marks a tissue tile, 0 background; the share of tissue differs from region to region of the grid. `decay_row`: decays lie in (0, 1], most close to one. `decay_col`: decays lie in (0, 1], most close to one.
All inputs are finite; a program needn't handle non-finite values.
Results may differ from the reference program's by a relative error of at most 0.011.
Values sent between devices are 32-bit elements; how exact they have to be, the bound alone decides.
A program may use at most 128 MiB of HBM per device.

```python
import math
import jax
import jax.numpy as jnp
from jax import lax

D = 512
HIDDEN_FEATURE = 1024
N = 16
RD = 16
CD = 8
TILE_DOWN = 64
TILE_ACROSS = 32


def decay_field(key, sequence_count, reach_low, reach_high):
    influence_seed_handle, jagged_seed_handle, jolt_seed_handle, objective_seed_handle = jax.random.split(key, 4)
    log_reach = jax.random.uniform(influence_seed_handle, (HIDDEN_FEATURE,), jnp.float32, math.log(reach_low), math.log(reach_high))
    influence_span = jnp.exp(log_reach)
    jaggedness_level = jax.random.uniform(jagged_seed_handle, (TILE_DOWN, TILE_ACROSS, HIDDEN_FEATURE), jnp.float32, 0.5, 2.0)
    jolt_magnitude = jax.random.bernoulli(jolt_seed_handle, 3.0 / sequence_count, (TILE_DOWN, TILE_ACROSS, HIDDEN_FEATURE))
    objective_summed = jax.random.uniform(objective_seed_handle, (TILE_DOWN, TILE_ACROSS, HIDDEN_FEATURE), jnp.float32, 0.2, 0.5)
    fading_multiplier = jnp.exp(-jaggedness_level / influence_span[None, None, :]) * jnp.where(jolt_magnitude, 1.0 - objective_summed, 1.0)
    return fading_multiplier.astype(jnp.bfloat16)


def draw_decay_row(key, part):
    sub_key = jax.random.fold_in(key, 11)
    return decay_field(sub_key, TILE_ACROSS, 30.0, 4.0 * TILE_ACROSS)


def draw_decay_col(key, part):
    sub_key = jax.random.fold_in(key, 23)
    return decay_field(sub_key, TILE_DOWN, 30.0, 4.0 * TILE_DOWN)


def draw_tissue(key, part):
    key_level, key_cell = jax.random.split(jax.random.fold_in(key, 37))
    raw_levels = jax.random.randint(key_level, (TILE_DOWN // RD, TILE_ACROSS // CD), 0, 4)
    levels = jnp.where(raw_levels == 3, 5, jnp.minimum(raw_levels, 1))
    spread_levels = jnp.repeat(jnp.repeat(levels, RD, axis=0), CD, axis=1)
    cells = jax.random.randint(key_cell, (TILE_DOWN, TILE_ACROSS), 0, 5)
    return (cells < spread_levels).astype(jnp.int32)


def block_levels(own_key, dims, cuts, least, largest):
    def one(axis_at, parts):
        steps = jax.random.uniform(jax.random.fold_in(jax.random.fold_in(own_key, 6), axis_at), (parts,), jnp.float32, least / len(cuts), largest / len(cuts))
        return jnp.repeat(jnp.exp(steps), dims[axis_at] // parts).reshape((-1,) + (1,) * (len(dims) - axis_at - 1))

    factor_of = one(*cuts[0])
    for cut in cuts[1:]:
        factor_of = factor_of * one(*cut)
    return factor_of


def normal_values(own_key, dims, deviation, most, cuts=(), kind=jnp.bfloat16):
    gain = block_levels(own_key, dims, cuts, -0.22, 0.18) if cuts else 1.0
    values = jax.random.normal(own_key, dims, jnp.float32) * deviation * gain
    return jnp.minimum(jnp.maximum(values, -most), most).astype(kind)


def setup_inputs(seed: int = 0, part: int = 0) -> dict:
    arg_keys = jax.random.split(jax.random.key(seed), 10)
    part_keys = jax.random.split(jax.random.fold_in(arg_keys[9], part), 10)
    features = normal_values(part_keys[0], (TILE_DOWN, TILE_ACROSS, D), 1.0, 6.0, ((0, 4), (1, 4)))
    out_grad = normal_values(part_keys[1], (TILE_DOWN, TILE_ACROSS, D), 1.0, 6.0, ((0, 4), (1, 4)))
    w_in = normal_values(arg_keys[2], (D, HIDDEN_FEATURE), D ** -0.5, 0.25)
    w_out = normal_values(arg_keys[3], (HIDDEN_FEATURE, D), HIDDEN_FEATURE ** -0.5, 0.1875)
    decay_row = draw_decay_row(jax.random.fold_in(jax.random.fold_in(arg_keys[9], part), 71), part)
    decay_col = draw_decay_col(jax.random.fold_in(jax.random.fold_in(arg_keys[9], part), 71), part)
    b_proj = normal_values(part_keys[6], (TILE_DOWN, TILE_ACROSS, N), 1.0, 6.0, ((0, 4), (1, 4)), jnp.float32)
    c_proj = normal_values(part_keys[7], (TILE_DOWN, TILE_ACROSS, N), 1.0, 6.0, ((0, 4), (1, 4)), jnp.float32)
    tissue = draw_tissue(jax.random.fold_in(jax.random.fold_in(arg_keys[9], part), 71), part)
    return dict(features=features, out_grad=out_grad, w_in=w_in, w_out=w_out, decay_row=decay_row, decay_col=decay_col, b_proj=b_proj, c_proj=c_proj, tissue=tissue)


def linear_step(carry_state, inputs):
    decay_now, source_now = inputs
    updated = decay_now * carry_state + source_now
    return (updated, updated)

def run_scan(fading_multiplier, source, axis, backwards):
    moved_decay = jnp.moveaxis(fading_multiplier, axis, 0)
    moved_source = jnp.moveaxis(source, axis, 0)
    start_state = jnp.zeros(moved_source.shape[1:], jnp.float32)
    final_state, states = lax.scan(linear_step, start_state, (moved_decay, moved_source), reverse=backwards)
    return jnp.moveaxis(states, 0, axis)

def block_grads(signal_blk, upstream_blk, row_decay, col_decay, b_proj, c_proj, norm_scale):
    row_dec4 = row_decay[:, :, None, :]
    col_dec4 = col_decay[:, :, None, :]
    source = norm_scale * b_proj[:, :, :, None] * signal_blk[:, :, None, :]
    row_state = run_scan(row_dec4, source, 1, False)
    col_state = run_scan(col_dec4, row_state, 0, False)
    mixed = lax.optimization_barrier(jnp.sum(c_proj[:, :, :, None] * col_state, axis=2))
    injected = c_proj[:, :, :, None] * upstream_blk[:, :, None, :]
    col_next = jnp.concatenate([col_dec4[1:], jnp.ones_like(col_dec4[:1])], axis=0)
    col_adj = run_scan(col_next, injected, 0, True)
    row_next = jnp.concatenate([row_dec4[:, 1:], jnp.ones_like(row_dec4[:, :1])], axis=1)
    row_adj = run_scan(row_next, col_adj, 1, True)
    row_prev = jnp.concatenate([jnp.zeros_like(row_state[:, :1]), row_state[:, :-1]], axis=1)
    col_prev = jnp.concatenate([jnp.zeros_like(col_state[:1]), col_state[:-1]], axis=0)
    row_dgrad = lax.optimization_barrier(jnp.sum(row_adj * row_prev, axis=2))
    col_dgrad = lax.optimization_barrier(jnp.sum(col_adj * col_prev, axis=2))
    signal_part = norm_scale * lax.optimization_barrier(jnp.sum(b_proj[:, :, :, None] * row_adj, axis=2))
    b_part = norm_scale * lax.optimization_barrier(jnp.sum(signal_blk[:, :, None, :] * row_adj, axis=3))
    c_part = lax.optimization_barrier(jnp.sum(upstream_blk[:, :, None, :] * col_state, axis=3))
    return (mixed, signal_part, row_dgrad, col_dgrad, b_part, c_part)

def reference(features, out_grad, w_in, w_out, decay_row, decay_col, b_proj, c_proj, tissue):
    height, width_cells = tissue.shape
    model_width = features.shape[2]
    inner = w_in.shape[1]
    norm_scale = 1.0 / math.sqrt(height * width_cells)
    feat_rows = features.reshape(height * width_cells, model_width)
    grad_rows = out_grad.reshape(height * width_cells, model_width)
    tissue_keep = tissue.astype(jnp.float32)[:, :, None]
    projected = jnp.dot(feat_rows, w_in, preferred_element_type=jnp.float32).reshape(height, width_cells, inner)
    signal = (tissue_keep * projected).astype(jnp.bfloat16)
    upstream = jnp.dot(grad_rows, w_out.T, preferred_element_type=jnp.float32).reshape(height, width_cells, inner).astype(jnp.bfloat16)
    channel_block = min(128, inner)
    mixed_parts, signal_parts, row_parts, col_parts = ([], [], [], [])
    b_grad = jnp.zeros(b_proj.shape, jnp.float32)
    c_grad = jnp.zeros(c_proj.shape, jnp.float32)
    for offset in range(0, inner, channel_block):
        window = slice(offset, offset + channel_block)
        outcome = block_grads(signal[:, :, window].astype(jnp.float32), upstream[:, :, window].astype(jnp.float32), decay_row[:, :, window].astype(jnp.float32), decay_col[:, :, window].astype(jnp.float32), b_proj, c_proj, norm_scale)
        mixed_parts.append(outcome[0])
        signal_parts.append(outcome[1])
        row_parts.append(outcome[2])
        col_parts.append(outcome[3])
        b_grad = b_grad + outcome[4]
        c_grad = c_grad + outcome[5]
    mixed = jnp.concatenate(mixed_parts, axis=2).astype(jnp.bfloat16)
    signal_grad = (tissue_keep * jnp.concatenate(signal_parts, axis=2)).astype(jnp.bfloat16)
    grad_flat = signal_grad.reshape(height * width_cells, inner)
    feat_grad = jnp.dot(grad_flat, w_in.T, preferred_element_type=jnp.float32).astype(jnp.bfloat16).reshape(height, width_cells, model_width)
    w_in_grad = jnp.dot(feat_rows.T, grad_flat, preferred_element_type=jnp.float32)
    w_out_grad = jnp.dot(mixed.reshape(height * width_cells, inner).T, grad_rows, preferred_element_type=jnp.float32)
    decay_row_grad = jnp.concatenate(row_parts, axis=2)
    decay_col_grad = jnp.concatenate(col_parts, axis=2)
    return (feat_grad, w_in_grad, w_out_grad, decay_row_grad, decay_col_grad, b_grad, c_grad)
```

```python
import functools
import math

import jax
import jax.numpy as jnp
from jax import lax
from jax.experimental import pallas as pl
from jax.experimental.pallas import tpu as pltpu
from jax.sharding import PartitionSpec as P

LANES = 128
F32 = jnp.float32


def place(shape):
    return lax.broadcasted_iota(jnp.int32, shape, 0)


def ahead_weights(decay):
    count = decay.shape[0]
    where = place(decay.shape)
    product, steps, shift = decay, [], 1
    while shift < count:
        inside = where >= shift
        steps.append((shift, jnp.where(inside, product, 0.0)))
        product = jnp.where(inside, product * pltpu.roll(product, shift, 0), product)
        shift *= 2
    return steps, product


def back_weights(decay):
    count = decay.shape[0]
    where = place(decay.shape)
    product = jnp.where(where == count - 1, 1.0, pltpu.roll(decay, count - 1, 0))
    steps, shift = [], 1
    while shift < count:
        inside = where < count - shift
        steps.append((count - shift, jnp.where(inside, product, 0.0)))
        product = jnp.where(inside, product * pltpu.roll(product, count - shift, 0), product)
        shift *= 2
    return steps, product


def run_scan(steps, value):
    for shift, weight in steps:
        value = value + weight * pltpu.roll(value, shift, 0)
    return value


def spread(source_ref, target_ref, scale):
    rows, cols, states = source_ref.shape

    def one(i, carry):
        block = source_ref[i] * scale
        for n in range(states):
            target_ref[i, n] = jnp.broadcast_to(block[:, n : n + 1], (cols, LANES))
        return carry

    lax.fori_loop(0, rows, one, 0)


def totals_kernel(scale, signal, upstream, row_decay, col_decay, b_proj, c_proj,
                  row_tot, row_prod, col_tot, col_prod, b_wide, c_wide):
    rows, cols, states = b_proj.shape

    @pl.when(pl.program_id(0) == 0)
    def _():
        spread(b_proj, b_wide, scale)
        spread(c_proj, c_wide, 1.0)

    def one(turn, carry):
        i = rows - 1 - turn
        product, adjoints = carry[0], carry[1:]
        down = col_decay[i]
        up = upstream[i]
        suffix = back_weights(row_decay[i])[1]
        weighted = suffix * signal[i]
        updated = []
        for n in range(states):
            updated.append(down * (adjoints[n] + c_wide[i, n] * up))
            row_tot[i, n : n + 1, :] = jnp.sum(b_wide[i, n] * weighted, axis=0, keepdims=True)
        row_prod[i] = row_decay[i][0:1] * suffix[0:1]
        return (product * down, *updated)

    ones = jnp.ones((cols, LANES), F32)
    zeros = jnp.zeros((cols, LANES), F32)
    out = lax.fori_loop(0, rows, one, (ones,) + (zeros,) * states)
    col_prod[...] = out[0]
    for n in range(states):
        col_tot[n] = out[1 + n]


def states_kernel(scale, signal, upstream, row_decay, col_decay, b_proj, c_proj, row_in, back_in,
                  row_state, col_adj, col_tot, back_tot, b_wide, c_wide):
    rows, cols, states = b_proj.shape

    @pl.when(pl.program_id(0) == 0)
    def _():
        spread(b_proj, b_wide, scale)
        spread(c_proj, c_wide, 1.0)

    def back(turn, entering):
        i = rows - 1 - turn
        down = col_decay[i]
        up = upstream[i]
        prefix_weight = ahead_weights(row_decay[i])[1]
        updated = []
        for n in range(states):
            adjoint = entering[n] + c_wide[i, n] * up
            col_adj[i, n] = adjoint
            back_tot[i, n : n + 1, :] = jnp.sum(prefix_weight * adjoint, axis=0, keepdims=True)
            updated.append(down * adjoint)
        return tuple(updated)

    lax.fori_loop(0, rows, back, tuple(back_in[n] for n in range(states)))

    def ahead(i, column):
        down = col_decay[i]
        source = signal[i]
        steps, product = ahead_weights(row_decay[i])
        updated = []
        for n in range(states):
            state = run_scan(steps, b_wide[i, n] * source) + product * row_in[i, n : n + 1, :]
            row_state[i, n] = state
            updated.append(down * column[n] + state)
        return tuple(updated)

    zeros = jnp.zeros((cols, LANES), F32)
    out = lax.fori_loop(0, rows, ahead, (zeros,) * states)
    for n in range(states):
        col_tot[n] = out[n]


def outputs_kernel(scale, signal, upstream, row_decay, col_decay, b_proj, c_proj,
                   row_state, col_adj, row_in, col_in, row_back,
                   mixed, signal_part, row_grad, col_grad, b_grad, c_grad,
                   b_wide, c_wide, b_sum, c_sum):
    rows, cols, states = b_proj.shape

    @pl.when(pl.program_id(0) == 0)
    def _():
        spread(b_proj, b_wide, scale)
        spread(c_proj, c_wide, 1.0)
        b_sum[...] = jnp.zeros_like(b_sum)
        c_sum[...] = jnp.zeros_like(c_sum)

    def one(i, column):
        down = col_decay[i]
        source = signal[i]
        up = upstream[i]
        steps, product = back_weights(row_decay[i])
        first = place((cols, LANES)) == 0
        mixed_now = jnp.zeros((cols, LANES), F32)
        signal_now, row_now, col_now = mixed_now, mixed_now, mixed_now
        updated = []
        for n in range(states):
            state = row_state[i, n]
            adjoint = col_adj[i, n]
            col_now = col_now + adjoint * column[n]
            fresh = down * column[n] + state
            updated.append(fresh)
            mixed_now = mixed_now + c_wide[i, n] * fresh
            c_sum[i, n] += up * fresh
            row_adj = run_scan(steps, adjoint) + product * row_back[i, n : n + 1, :]
            before = jnp.where(first, row_in[i, n : n + 1, :], pltpu.roll(state, 1, 0))
            row_now = row_now + row_adj * before
            signal_now = signal_now + b_wide[i, n] * row_adj
            b_sum[i, n] += source * row_adj
        mixed[i] = mixed_now
        signal_part[i] = signal_now
        row_grad[i] = row_now
        col_grad[i] = col_now
        return tuple(updated)

    lax.fori_loop(0, rows, one, tuple(col_in[n] for n in range(states)))

    @pl.when(pl.program_id(0) == pl.num_programs(0) - 1)
    def _():
        def finish(i, carry):
            for n in range(states):
                b_grad[i, :, n : n + 1] = scale * jnp.sum(b_sum[i, n], axis=1, keepdims=True)
                c_grad[i, :, n : n + 1] = jnp.sum(c_sum[i, n], axis=1, keepdims=True)
            return carry

        lax.fori_loop(0, rows, finish, 0)


def tile(shape):
    zeros = (0,) * (len(shape) - 1)
    return pl.BlockSpec((*shape[:-1], LANES), lambda t: (*zeros, t))


def whole(shape):
    zeros = (0,) * len(shape)
    return pl.BlockSpec(shape, lambda t: zeros)


def call(kernel, name, scale, args, kept, outs, kept_outs, scratch):
    return pl.pallas_call(
        functools.partial(kernel, scale),
        grid=(args[0].shape[-1] // LANES,),
        in_specs=[whole(a.shape) if k in kept else tile(a.shape) for k, a in enumerate(args)],
        out_specs=[whole(o) if k in kept_outs else tile(o) for k, o in enumerate(outs)],
        out_shape=[jax.ShapeDtypeStruct(o, F32) for o in outs],
        scratch_shapes=[pltpu.VMEM(s, F32) for s in scratch],
        compiler_params=pltpu.CompilerParams(vmem_limit_bytes=40 * 2**20),
        name=name,
    )(*args)


def entering(total, product, axis, reverse):
    count = lax.axis_size(axis)
    me = lax.axis_index(axis)
    totals = lax.all_gather(total, axis)
    products = lax.all_gather(product, axis)
    state = jnp.zeros_like(total)
    for turn in range(count - 1):
        k = count - 1 - turn if reverse else turn
        use = k > me if reverse else k < me
        state = jnp.where(use, products[k] * state + totals[k], state)
    return state


def shards(features, out_grad, w_in, w_out, decay_row, decay_col, b_proj, c_proj, tissue):
    rows, cols, width = features.shape
    inner = w_in.shape[1]
    states = b_proj.shape[2]
    cells = rows * cols
    scale = 1.0 / math.sqrt(cells * lax.axis_size("gr") * lax.axis_size("gc"))
    feat = features.reshape(cells, width)
    grad = out_grad.reshape(cells, width)
    keep = tissue.astype(F32)[:, :, None]
    contract_last = (((1,), (1,)), ((), ()))
    contract_first = (((0,), (0,)), ((), ()))
    projected = jnp.dot(feat, w_in, preferred_element_type=F32).reshape(rows, cols, inner)
    signal = (keep * projected).astype(jnp.bfloat16).astype(F32)
    upstream = lax.dot_general(grad, w_out, contract_last, preferred_element_type=F32)
    upstream = upstream.astype(jnp.bfloat16).astype(F32).reshape(rows, cols, inner)
    common = (signal, upstream, decay_row.astype(F32), decay_col.astype(F32), b_proj, c_proj)

    cell = (rows, cols, inner)
    row_edge = (rows, states, inner)
    col_edge = (states, cols, inner)
    full = (rows, states, cols, inner)
    wide = (rows, states, cols, LANES)
    row_tot, row_prod, col_back_tot, col_prod = call(
        totals_kernel, "totals", scale, common, (4, 5),
        (row_edge, (rows, 1, inner), col_edge, (cols, inner)), (), (wide, wide),
    )
    row_in = entering(row_tot, row_prod, "gc", False)
    col_back = entering(col_back_tot, col_prod, "gr", True)
    row_state, col_adj, col_tot, row_back_tot = call(
        states_kernel, "states", scale, (*common, row_in, col_back), (4, 5),
        (full, full, col_edge, row_edge), (), (wide, wide),
    )
    col_in = entering(col_tot, col_prod, "gr", False)
    row_back = entering(row_back_tot, row_prod, "gc", True)
    mixed, signal_part, row_grad, col_grad, b_grad, c_grad = call(
        outputs_kernel, "outputs", scale,
        (*common, row_state, col_adj, row_in, col_in, row_back), (4, 5),
        (cell, cell, cell, cell, b_proj.shape, c_proj.shape), (4, 5), (wide, wide, wide, wide),
    )
    mixed = mixed.astype(jnp.bfloat16).reshape(cells, inner)
    signal_grad = (keep * signal_part).astype(jnp.bfloat16).reshape(cells, inner)
    feat_grad = lax.dot_general(signal_grad, w_in, contract_last, preferred_element_type=F32)
    feat_grad = feat_grad.astype(jnp.bfloat16).reshape(rows, cols, width)
    w_in_part = lax.dot_general(feat, signal_grad, contract_first, preferred_element_type=F32)
    w_out_part = lax.dot_general(mixed, grad, contract_first, preferred_element_type=F32)
    w_in_grad, w_out_grad = lax.psum((w_in_part, w_out_part), ("gr", "gc"))
    return (feat_grad, w_in_grad, w_out_grad, row_grad, col_grad, b_grad, c_grad)


def solution(mesh):
    cell = P(("slide", "gr"), "gc", None)
    in_specs = (cell, cell, P(), P(), cell, cell, cell, cell, P(("slide", "gr"), "gc"))
    out_specs = (cell, P("slide", None), P("slide", None), cell, cell, cell, cell)
    return jax.shard_map(shards, mesh=mesh, in_specs=in_specs, out_specs=out_specs, check_vma=False)
```

```python
import functools
import math

import jax
import jax.numpy as jnp
from jax import lax
from jax.experimental import pallas as pl
from jax.experimental.pallas import tpu as pltpu
from jax.sharding import PartitionSpec as P

LANES = 128
CHUNKS = 8
MESH = pl.DeviceIdType.MESH
F32 = jnp.float32


def place(shape):
    return lax.broadcasted_iota(jnp.int32, shape, 0)


def ahead_weights(decay):
    count = decay.shape[0]
    where = place(decay.shape)
    product, steps, shift = decay, [], 1
    while shift < count:
        inside = where >= shift
        steps.append((shift, jnp.where(inside, product, 0.0)))
        product = jnp.where(inside, product * pltpu.roll(product, shift, 0), product)
        shift *= 2
    return steps, product


def back_weights(decay):
    count = decay.shape[0]
    where = place(decay.shape)
    product = jnp.where(where == count - 1, 1.0, pltpu.roll(decay, count - 1, 0))
    steps, shift = [], 1
    while shift < count:
        inside = where < count - shift
        steps.append((count - shift, jnp.where(inside, product, 0.0)))
        product = jnp.where(inside, product * pltpu.roll(product, count - shift, 0), product)
        shift *= 2
    return steps, product


def run_scan(steps, value):
    for shift, weight in steps:
        value = value + weight * pltpu.roll(value, shift, 0)
    return value


def spread(source_ref, target_ref, scale):
    rows, cols, states = source_ref.shape

    def one(i, carry):
        block = source_ref[i] * scale
        for n in range(states):
            target_ref[i, n] = jnp.broadcast_to(block[:, n : n + 1], (cols, LANES))
        return carry

    lax.fori_loop(0, rows, one, 0)


def totals_kernel(scale, signal, upstream, row_decay, col_decay, b_proj, c_proj,
                  row_tot, row_prod, col_tot, col_prod, b_wide, c_wide):
    rows, cols, states = b_proj.shape

    @pl.when(pl.program_id(0) == 0)
    def _():
        spread(b_proj, b_wide, scale)
        spread(c_proj, c_wide, 1.0)

    def one(turn, carry):
        i = rows - 1 - turn
        product, adjoints = carry[0], carry[1:]
        down = col_decay[i]
        up = upstream[i]
        suffix = back_weights(row_decay[i])[1]
        weighted = suffix * signal[i]
        updated = []
        for n in range(states):
            updated.append(down * (adjoints[n] + c_wide[i, n] * up))
            row_tot[i, n : n + 1, :] = jnp.sum(b_wide[i, n] * weighted, axis=0, keepdims=True)
        row_prod[i] = row_decay[i][0:1] * suffix[0:1]
        return (product * down, *updated)

    ones = jnp.ones((cols, LANES), F32)
    zeros = jnp.zeros((cols, LANES), F32)
    out = lax.fori_loop(0, rows, one, (ones,) + (zeros,) * states)
    col_prod[...] = out[0]
    for n in range(states):
        col_tot[n] = out[1 + n]


def states_kernel(scale, signal, upstream, row_decay, col_decay, b_proj, c_proj, row_in, back_in,
                  row_state, col_adj, col_tot, back_tot, b_wide, c_wide):
    rows, cols, states = b_proj.shape

    @pl.when(pl.program_id(0) == 0)
    def _():
        spread(b_proj, b_wide, scale)
        spread(c_proj, c_wide, 1.0)

    def back(turn, entering):
        i = rows - 1 - turn
        down = col_decay[i]
        up = upstream[i]
        prefix_weight = ahead_weights(row_decay[i])[1]
        updated = []
        for n in range(states):
            adjoint = entering[n] + c_wide[i, n] * up
            col_adj[i, n] = adjoint
            back_tot[i, n : n + 1, :] = jnp.sum(prefix_weight * adjoint, axis=0, keepdims=True)
            updated.append(down * adjoint)
        return tuple(updated)

    lax.fori_loop(0, rows, back, tuple(back_in[n] for n in range(states)))

    def ahead(i, column):
        down = col_decay[i]
        source = signal[i]
        steps, product = ahead_weights(row_decay[i])
        updated = []
        for n in range(states):
            state = run_scan(steps, b_wide[i, n] * source) + product * row_in[i, n : n + 1, :]
            row_state[i, n] = state
            updated.append(down * column[n] + state)
        return tuple(updated)

    zeros = jnp.zeros((cols, LANES), F32)
    out = lax.fori_loop(0, rows, ahead, (zeros,) * states)
    for n in range(states):
        col_tot[n] = out[n]


def outputs_kernel(scale, signal, upstream, row_decay, col_decay, b_proj, c_proj,
                   row_state, col_adj, row_in, col_in, row_back,
                   mixed, signal_part, row_grad, col_grad, b_grad, c_grad,
                   b_wide, c_wide, b_sum, c_sum):
    rows, cols, states = b_proj.shape

    @pl.when(pl.program_id(0) == 0)
    def _():
        spread(b_proj, b_wide, scale)
        spread(c_proj, c_wide, 1.0)
        b_sum[...] = jnp.zeros_like(b_sum)
        c_sum[...] = jnp.zeros_like(c_sum)

    def one(i, column):
        down = col_decay[i]
        source = signal[i]
        up = upstream[i]
        steps, product = back_weights(row_decay[i])
        first = place((cols, LANES)) == 0
        mixed_now = jnp.zeros((cols, LANES), F32)
        signal_now, row_now, col_now = mixed_now, mixed_now, mixed_now
        updated = []
        for n in range(states):
            state = row_state[i, n]
            adjoint = col_adj[i, n]
            col_now = col_now + adjoint * column[n]
            fresh = down * column[n] + state
            updated.append(fresh)
            mixed_now = mixed_now + c_wide[i, n] * fresh
            c_sum[i, n] += up * fresh
            row_adj = run_scan(steps, adjoint) + product * row_back[i, n : n + 1, :]
            before = jnp.where(first, row_in[i, n : n + 1, :], pltpu.roll(state, 1, 0))
            row_now = row_now + row_adj * before
            signal_now = signal_now + b_wide[i, n] * row_adj
            b_sum[i, n] += source * row_adj
        mixed[i] = mixed_now
        signal_part[i] = signal_now
        row_grad[i] = row_now
        col_grad[i] = col_now
        return tuple(updated)

    lax.fori_loop(0, rows, one, tuple(col_in[n] for n in range(states)))

    @pl.when(pl.program_id(0) == pl.num_programs(0) - 1)
    def _():
        def finish(i, carry):
            for n in range(states):
                b_grad[i, :, n : n + 1] = scale * jnp.sum(b_sum[i, n], axis=1, keepdims=True)
                c_grad[i, :, n : n + 1] = jnp.sum(c_sum[i, n], axis=1, keepdims=True)
            return carry

        lax.fori_loop(0, rows, finish, 0)


def tile(shape):
    zeros = (0,) * (len(shape) - 1)
    return pl.BlockSpec((*shape[:-1], LANES), lambda t: (*zeros, t))


def whole(shape):
    zeros = (0,) * len(shape)
    return pl.BlockSpec(shape, lambda t: zeros)


def call(kernel, name, scale, args, kept, outs, kept_outs, scratch):
    return pl.pallas_call(
        functools.partial(kernel, scale),
        grid=(args[0].shape[-1] // LANES,),
        in_specs=[whole(a.shape) if k in kept else tile(a.shape) for k, a in enumerate(args)],
        out_specs=[whole(o) if k in kept_outs else tile(o) for k, o in enumerate(outs)],
        out_shape=[jax.ShapeDtypeStruct(o, F32) for o in outs],
        scratch_shapes=[pltpu.VMEM(s, F32) for s in scratch],
        compiler_params=pltpu.CompilerParams(vmem_limit_bytes=40 * 2**20),
        name=name,
    )(*args)


def chain_of(axis, step):
    count = lax.axis_size(axis)
    me = lax.axis_index(axis)
    turn = me if step > 0 else count - 1 - me
    after = lax.rem(me + step + count, count)
    before = lax.rem(me - step + count, count)
    return turn > 0, turn < count - 1, before, after


def exchange_kernel(row_step, col_step, row_tot, row_prod, col_tot, col_prod, row_in, col_in,
                    row_out, col_out, row_send, row_recv, col_send, col_recv):
    row_has_before, row_has_after, row_before, row_after = chain_of("gc", row_step)
    col_has_before, col_has_after, col_before, col_after = chain_of("gr", col_step)
    barrier = pltpu.get_barrier_semaphore()

    @pl.when(row_has_before)
    def _():
        pl.semaphore_signal(barrier, inc=1, device_id={"gc": row_before}, device_id_type=MESH)

    @pl.when(col_has_before)
    def _():
        pl.semaphore_signal(barrier, inc=1, device_id={"gr": col_before}, device_id_type=MESH)

    peers = row_has_after.astype(jnp.int32) + col_has_after.astype(jnp.int32)

    @pl.when(peers > 0)
    def _():
        pl.semaphore_wait(barrier, peers)

    row_part = row_tot.shape[0] // CHUNKS
    col_part = col_tot.shape[0] // CHUNKS

    def row_copy(k):
        part = pl.ds(k * row_part, row_part)
        return pltpu.make_async_remote_copy(
            src_ref=row_out.at[part], dst_ref=row_in.at[part],
            send_sem=row_send.at[k], recv_sem=row_recv.at[k],
            device_id={"gc": row_after}, device_id_type=MESH,
        )

    def col_copy(k):
        part = pl.ds(k * col_part, col_part)
        return pltpu.make_async_remote_copy(
            src_ref=col_out.at[part], dst_ref=col_in.at[part],
            send_sem=col_send.at[k], recv_sem=col_recv.at[k],
            device_id={"gr": col_after}, device_id_type=MESH,
        )

    @pl.when(jnp.logical_not(row_has_before))
    def _():
        row_in[...] = jnp.zeros_like(row_in)

    @pl.when(jnp.logical_not(col_has_before))
    def _():
        col_in[...] = jnp.zeros_like(col_in)

    def one(k, carry):
        @pl.when(col_has_before)
        def _():
            col_copy(k).wait_recv()

        @pl.when(col_has_after)
        def _():
            for p in range(col_part):
                n = k * col_part + p
                col_out[n] = col_prod[...] * col_in[n] + col_tot[n]
            col_copy(k).start()

        @pl.when(row_has_before)
        def _():
            row_copy(k).wait_recv()

        @pl.when(row_has_after)
        def _():
            for p in range(row_part):
                i = k * row_part + p
                row_out[i] = row_prod[i] * row_in[i] + row_tot[i]
            row_copy(k).start()

        return carry

    lax.fori_loop(0, CHUNKS, one, 0)

    def finish(k, carry):
        @pl.when(col_has_after)
        def _():
            col_copy(k).wait_send()

        @pl.when(row_has_after)
        def _():
            row_copy(k).wait_send()

        return carry

    lax.fori_loop(0, CHUNKS, finish, 0)


def exchange(name, number, row_step, col_step, row_tot, row_prod, col_tot, col_prod):
    vmem = pl.BlockSpec(memory_space=pltpu.VMEM)
    return pl.pallas_call(
        functools.partial(exchange_kernel, row_step, col_step),
        out_shape=[
            jax.ShapeDtypeStruct(row_tot.shape, F32), jax.ShapeDtypeStruct(col_tot.shape, F32)
        ],
        in_specs=[vmem] * 4,
        out_specs=[vmem] * 2,
        scratch_shapes=[pltpu.VMEM(row_tot.shape, F32), pltpu.VMEM(col_tot.shape, F32)]
        + [pltpu.SemaphoreType.DMA((CHUNKS,))] * 4,
        compiler_params=pltpu.CompilerParams(
            collective_id=number, has_side_effects=True, vmem_limit_bytes=32 * 2**20
        ),
        name=name,
    )(row_tot, row_prod, col_tot, col_prod)


def shards(features, out_grad, w_in, w_out, decay_row, decay_col, b_proj, c_proj, tissue):
    rows, cols, width = features.shape
    inner = w_in.shape[1]
    states = b_proj.shape[2]
    cells = rows * cols
    scale = 1.0 / math.sqrt(cells * lax.axis_size("gr") * lax.axis_size("gc"))
    feat = features.reshape(cells, width)
    grad = out_grad.reshape(cells, width)
    keep = tissue.astype(F32)[:, :, None]
    contract_last = (((1,), (1,)), ((), ()))
    contract_first = (((0,), (0,)), ((), ()))
    projected = jnp.dot(feat, w_in, preferred_element_type=F32).reshape(rows, cols, inner)
    signal = (keep * projected).astype(jnp.bfloat16).astype(F32)
    upstream = lax.dot_general(grad, w_out, contract_last, preferred_element_type=F32)
    upstream = upstream.astype(jnp.bfloat16).astype(F32).reshape(rows, cols, inner)
    common = (signal, upstream, decay_row.astype(F32), decay_col.astype(F32), b_proj, c_proj)

    cell = (rows, cols, inner)
    row_edge = (rows, states, inner)
    col_edge = (states, cols, inner)
    full = (rows, states, cols, inner)
    wide = (rows, states, cols, LANES)
    row_tot, row_prod, col_back_tot, col_prod = call(
        totals_kernel, "totals", scale, common, (4, 5),
        (row_edge, (rows, 1, inner), col_edge, (cols, inner)), (), (wide, wide),
    )
    row_in, col_back = exchange(
        "exchange_one", 0, 1, -1, row_tot, row_prod, col_back_tot, col_prod
    )
    row_state, col_adj, col_tot, row_back_tot = call(
        states_kernel, "states", scale, (*common, row_in, col_back), (4, 5),
        (full, full, col_edge, row_edge), (), (wide, wide),
    )
    row_back, col_in = exchange(
        "exchange_two", 1, -1, 1, row_back_tot, row_prod, col_tot, col_prod
    )
    mixed, signal_part, row_grad, col_grad, b_grad, c_grad = call(
        outputs_kernel, "outputs", scale,
        (*common, row_state, col_adj, row_in, col_in, row_back), (4, 5),
        (cell, cell, cell, cell, b_proj.shape, c_proj.shape), (4, 5), (wide, wide, wide, wide),
    )
    mixed = mixed.astype(jnp.bfloat16).reshape(cells, inner)
    signal_grad = (keep * signal_part).astype(jnp.bfloat16).reshape(cells, inner)
    feat_grad = lax.dot_general(signal_grad, w_in, contract_last, preferred_element_type=F32)
    feat_grad = feat_grad.astype(jnp.bfloat16).reshape(rows, cols, width)
    w_in_part = lax.dot_general(feat, signal_grad, contract_first, preferred_element_type=F32)
    w_out_part = lax.dot_general(mixed, grad, contract_first, preferred_element_type=F32)
    w_in_grad, w_out_grad = lax.psum((w_in_part, w_out_part), ("gr", "gc"))
    return (feat_grad, w_in_grad, w_out_grad, row_grad, col_grad, b_grad, c_grad)


def solution(mesh):
    cell = P(("slide", "gr"), "gc", None)
    in_specs = (cell, cell, P(), P(), cell, cell, cell, cell, P(("slide", "gr"), "gc"))
    out_specs = (cell, P("slide", None), P("slide", None), cell, cell, cell, cell)
    return jax.shard_map(shards, mesh=mesh, in_specs=in_specs, out_specs=out_specs, check_vma=False)
```

```python
import functools
import math

import jax
import jax.numpy as jnp
from jax import lax
from jax.experimental import pallas as pl
from jax.experimental.pallas import tpu as pltpu
from jax.sharding import PartitionSpec as P

LANES = 128
CHUNKS = 8
MESH = pl.DeviceIdType.MESH
F32 = jnp.float32


def place(shape):
    return lax.broadcasted_iota(jnp.int32, shape, 0)


def ahead_weights(decay):
    count = decay.shape[0]
    where = place(decay.shape)
    product, steps, shift = decay, [], 1
    while shift < count:
        inside = where >= shift
        steps.append((shift, jnp.where(inside, product, 0.0)))
        product = jnp.where(inside, product * pltpu.roll(product, shift, 0), product)
        shift *= 2
    return steps, product


def back_weights(decay):
    count = decay.shape[0]
    where = place(decay.shape)
    product = jnp.where(where == count - 1, 1.0, pltpu.roll(decay, count - 1, 0))
    steps, shift = [], 1
    while shift < count:
        inside = where < count - shift
        steps.append((count - shift, jnp.where(inside, product, 0.0)))
        product = jnp.where(inside, product * pltpu.roll(product, count - shift, 0), product)
        shift *= 2
    return steps, product


def run_scan(steps, value):
    for shift, weight in steps:
        value = value + weight * pltpu.roll(value, shift, 0)
    return value


def spread(source_ref, target_ref, scale):
    rows, cols, states = source_ref.shape

    def one(i, carry):
        block = source_ref[i] * scale
        for n in range(states):
            target_ref[i, n] = jnp.broadcast_to(block[:, n : n + 1], (cols, LANES))
        return carry

    lax.fori_loop(0, rows, one, 0)


def totals_kernel(scale, signal, upstream, row_decay, col_decay, b_proj, c_proj,
                  row_tot, row_prod, col_tot, col_prod, b_wide, c_wide):
    rows, cols, states = b_proj.shape

    @pl.when(pl.program_id(0) == 0)
    def _():
        spread(b_proj, b_wide, scale)
        spread(c_proj, c_wide, 1.0)

    def one(turn, carry):
        i = rows - 1 - turn
        product, adjoints = carry[0], carry[1:]
        down = col_decay[i]
        up = upstream[i]
        suffix = back_weights(row_decay[i])[1]
        weighted = suffix * signal[i]
        updated = []
        for n in range(states):
            updated.append(down * (adjoints[n] + c_wide[i, n] * up))
            row_tot[i, n : n + 1, :] = jnp.sum(b_wide[i, n] * weighted, axis=0, keepdims=True)
        row_prod[i] = row_decay[i][0:1] * suffix[0:1]
        return (product * down, *updated)

    ones = jnp.ones((cols, LANES), F32)
    zeros = jnp.zeros((cols, LANES), F32)
    out = lax.fori_loop(0, rows, one, (ones,) + (zeros,) * states)
    col_prod[...] = out[0]
    for n in range(states):
        col_tot[n] = out[1 + n]


def states_kernel(scale, signal, upstream, row_decay, col_decay, b_proj, c_proj, row_in, back_in,
                  row_state, col_adj, col_tot, back_tot, b_wide, c_wide):
    rows, cols, states = b_proj.shape

    @pl.when(pl.program_id(0) == 0)
    def _():
        spread(b_proj, b_wide, scale)
        spread(c_proj, c_wide, 1.0)

    def back(turn, entering):
        i = rows - 1 - turn
        down = col_decay[i]
        up = upstream[i]
        prefix_weight = ahead_weights(row_decay[i])[1]
        updated = []
        for n in range(states):
            adjoint = entering[n] + c_wide[i, n] * up
            col_adj[i, n] = adjoint
            back_tot[i, n : n + 1, :] = jnp.sum(prefix_weight * adjoint, axis=0, keepdims=True)
            updated.append(down * adjoint)
        return tuple(updated)

    lax.fori_loop(0, rows, back, tuple(back_in[n] for n in range(states)))

    def ahead(i, column):
        down = col_decay[i]
        source = signal[i]
        steps, product = ahead_weights(row_decay[i])
        updated = []
        for n in range(states):
            state = run_scan(steps, b_wide[i, n] * source) + product * row_in[i, n : n + 1, :]
            row_state[i, n] = state
            updated.append(down * column[n] + state)
        return tuple(updated)

    zeros = jnp.zeros((cols, LANES), F32)
    out = lax.fori_loop(0, rows, ahead, (zeros,) * states)
    for n in range(states):
        col_tot[n] = out[n]


def col_outputs_kernel(scale, upstream, col_decay, c_proj, row_state, col_adj, col_in,
                       mixed, col_grad, c_grad, c_wide, c_sum):
    rows, cols, states = c_proj.shape

    @pl.when(pl.program_id(0) == 0)
    def _():
        spread(c_proj, c_wide, 1.0)
        c_sum[...] = jnp.zeros_like(c_sum)

    def one(i, column):
        down = col_decay[i]
        up = upstream[i]
        mixed_now = jnp.zeros((cols, LANES), F32)
        col_now = mixed_now
        updated = []
        for n in range(states):
            col_now = col_now + col_adj[i, n] * column[n]
            fresh = down * column[n] + row_state[i, n]
            updated.append(fresh)
            mixed_now = mixed_now + c_wide[i, n] * fresh
            c_sum[i, n] += up * fresh
        mixed[i] = mixed_now
        col_grad[i] = col_now
        return tuple(updated)

    lax.fori_loop(0, rows, one, tuple(col_in[n] for n in range(states)))

    @pl.when(pl.program_id(0) == pl.num_programs(0) - 1)
    def _():
        def finish(i, carry):
            for n in range(states):
                c_grad[i, :, n : n + 1] = jnp.sum(c_sum[i, n], axis=1, keepdims=True)
            return carry

        lax.fori_loop(0, rows, finish, 0)


def row_outputs_kernel(scale, signal, row_decay, b_proj, row_state, col_adj, row_in, row_back,
                       signal_part, row_grad, b_grad, b_wide, b_sum):
    rows, cols, states = b_proj.shape

    @pl.when(pl.program_id(0) == 0)
    def _():
        spread(b_proj, b_wide, scale)
        b_sum[...] = jnp.zeros_like(b_sum)

    def one(i, carry):
        source = signal[i]
        steps, product = back_weights(row_decay[i])
        first = place((cols, LANES)) == 0
        signal_now = jnp.zeros((cols, LANES), F32)
        row_now = signal_now
        for n in range(states):
            row_adj = run_scan(steps, col_adj[i, n]) + product * row_back[i, n : n + 1, :]
            before = jnp.where(first, row_in[i, n : n + 1, :], pltpu.roll(row_state[i, n], 1, 0))
            row_now = row_now + row_adj * before
            signal_now = signal_now + b_wide[i, n] * row_adj
            b_sum[i, n] += source * row_adj
        signal_part[i] = signal_now
        row_grad[i] = row_now
        return carry

    lax.fori_loop(0, rows, one, 0)

    @pl.when(pl.program_id(0) == pl.num_programs(0) - 1)
    def _():
        def finish(i, carry):
            for n in range(states):
                b_grad[i, :, n : n + 1] = scale * jnp.sum(b_sum[i, n], axis=1, keepdims=True)
            return carry

        lax.fori_loop(0, rows, finish, 0)


def tile(shape):
    zeros = (0,) * (len(shape) - 1)
    return pl.BlockSpec((*shape[:-1], LANES), lambda t: (*zeros, t))


def whole(shape):
    zeros = (0,) * len(shape)
    return pl.BlockSpec(shape, lambda t: zeros)


def call(kernel, name, scale, args, kept, outs, kept_outs, scratch):
    return pl.pallas_call(
        functools.partial(kernel, scale),
        grid=(args[0].shape[-1] // LANES,),
        in_specs=[whole(a.shape) if k in kept else tile(a.shape) for k, a in enumerate(args)],
        out_specs=[whole(o) if k in kept_outs else tile(o) for k, o in enumerate(outs)],
        out_shape=[jax.ShapeDtypeStruct(o, F32) for o in outs],
        scratch_shapes=[pltpu.VMEM(s, F32) for s in scratch],
        compiler_params=pltpu.CompilerParams(vmem_limit_bytes=40 * 2**20),
        name=name,
    )(*args)


def chain_of(axis, step):
    count = lax.axis_size(axis)
    me = lax.axis_index(axis)
    turn = me if step > 0 else count - 1 - me
    after = lax.rem(me + step + count, count)
    before = lax.rem(me - step + count, count)
    return turn > 0, turn < count - 1, before, after


def exchange_kernel(chains, *refs):
    count = len(chains)
    total, product = refs[0 : 2 * count : 2], refs[1 : 2 * count : 2]
    arrived = refs[2 * count : 3 * count]
    leaving = refs[3 * count : 4 * count]
    send, recv = refs[4 * count : 5 * count], refs[5 * count :]
    places = [chain_of(axis, step) for axis, step in chains]
    barrier = pltpu.get_barrier_semaphore()
    peers = 0
    for (axis, _), (has_before, has_after, before, _) in zip(chains, places):
        peers = peers + has_after.astype(jnp.int32)

        @pl.when(has_before)
        def _(axis=axis, before=before):
            pl.semaphore_signal(barrier, inc=1, device_id={axis: before}, device_id_type=MESH)

    @pl.when(peers > 0)
    def _():
        pl.semaphore_wait(barrier, peers)

    def copy(c, k):
        size = total[c].shape[0] // CHUNKS
        part = pl.ds(k * size, size)
        return pltpu.make_async_remote_copy(
            src_ref=leaving[c].at[part], dst_ref=arrived[c].at[part],
            send_sem=send[c].at[k], recv_sem=recv[c].at[k],
            device_id={chains[c][0]: places[c][3]}, device_id_type=MESH,
        )

    for c in range(count):

        @pl.when(jnp.logical_not(places[c][0]))
        def _(c=c):
            arrived[c][...] = jnp.zeros_like(arrived[c])

    def one(k, carry):
        for c in range(count):

            @pl.when(places[c][0])
            def _(c=c):
                copy(c, k).wait_recv()

            @pl.when(places[c][1])
            def _(c=c):
                size = total[c].shape[0] // CHUNKS
                for p in range(size):
                    i = k * size + p
                    weight = product[c][i] if len(product[c].shape) == 3 else product[c][...]
                    leaving[c][i] = weight * arrived[c][i] + total[c][i]
                copy(c, k).start()

        return carry

    lax.fori_loop(0, CHUNKS, one, 0)

    def finish(k, carry):
        for c in range(count):

            @pl.when(places[c][1])
            def _(c=c):
                copy(c, k).wait_send()

        return carry

    lax.fori_loop(0, CHUNKS, finish, 0)


def exchange(name, number, chains, *args):
    vmem = pl.BlockSpec(memory_space=pltpu.VMEM)
    shapes = [a.shape for a in args[::2]]
    return pl.pallas_call(
        functools.partial(exchange_kernel, chains),
        out_shape=[jax.ShapeDtypeStruct(a, F32) for a in shapes],
        in_specs=[vmem] * len(args),
        out_specs=[vmem] * len(shapes),
        scratch_shapes=[pltpu.VMEM(a, F32) for a in shapes]
        + [pltpu.SemaphoreType.DMA((CHUNKS,))] * (2 * len(shapes)),
        compiler_params=pltpu.CompilerParams(
            collective_id=number, has_side_effects=True, vmem_limit_bytes=32 * 2**20
        ),
        name=name,
    )(*args)


def shards(features, out_grad, w_in, w_out, decay_row, decay_col, b_proj, c_proj, tissue):
    rows, cols, width = features.shape
    inner = w_in.shape[1]
    states = b_proj.shape[2]
    cells = rows * cols
    scale = 1.0 / math.sqrt(cells * lax.axis_size("gr") * lax.axis_size("gc"))
    feat = features.reshape(cells, width)
    grad = out_grad.reshape(cells, width)
    keep = tissue.astype(F32)[:, :, None]
    contract_last = (((1,), (1,)), ((), ()))
    contract_first = (((0,), (0,)), ((), ()))
    projected = jnp.dot(feat, w_in, preferred_element_type=F32).reshape(rows, cols, inner)
    signal = (keep * projected).astype(jnp.bfloat16).astype(F32)
    upstream = lax.dot_general(grad, w_out, contract_last, preferred_element_type=F32)
    upstream = upstream.astype(jnp.bfloat16).astype(F32).reshape(rows, cols, inner)
    common = (signal, upstream, decay_row.astype(F32), decay_col.astype(F32), b_proj, c_proj)

    cell = (rows, cols, inner)
    row_edge = (rows, states, inner)
    col_edge = (states, cols, inner)
    full = (rows, states, cols, inner)
    wide = (rows, states, cols, LANES)
    row_tot, row_prod, col_back_tot, col_prod = call(
        totals_kernel, "totals", scale, common, (4, 5),
        (row_edge, (rows, 1, inner), col_edge, (cols, inner)), (), (wide, wide),
    )
    row_in, col_back = exchange(
        "exchange_one", 0, (("gc", 1), ("gr", -1)), row_tot, row_prod, col_back_tot, col_prod
    )
    row_state, col_adj, col_tot, row_back_tot = call(
        states_kernel, "states", scale, (*common, row_in, col_back), (4, 5),
        (full, full, col_edge, row_edge), (), (wide, wide),
    )
    (col_in,) = exchange("exchange_col", 1, (("gr", 1),), col_tot, col_prod)
    signal, upstream, row_decay, col_decay = common[:4]
    mixed, col_grad, c_grad = call(
        col_outputs_kernel, "col_outputs", scale,
        (upstream, col_decay, c_proj, row_state, col_adj, col_in), (2,),
        (cell, cell, c_proj.shape), (2,), (wide, wide),
    )
    mixed = mixed.astype(jnp.bfloat16).reshape(cells, inner)
    w_out_part = lax.dot_general(mixed, grad, contract_first, preferred_element_type=F32)
    w_out_part, row_back_tot = lax.optimization_barrier((w_out_part, row_back_tot))
    w_out_grad = lax.psum(w_out_part, ("gr", "gc"))
    (row_back,) = exchange("exchange_row", 2, (("gc", -1),), row_back_tot, row_prod)
    signal_part, row_grad, b_grad = call(
        row_outputs_kernel, "row_outputs", scale,
        (signal, row_decay, b_proj, row_state, col_adj, row_in, row_back), (2,),
        (cell, cell, b_proj.shape), (2,), (wide, wide),
    )
    signal_grad = (keep * signal_part).astype(jnp.bfloat16).reshape(cells, inner)
    w_in_part = lax.dot_general(feat, signal_grad, contract_first, preferred_element_type=F32)
    w_in_part, w_out_grad = lax.optimization_barrier((w_in_part, w_out_grad))
    w_in_grad = lax.psum(w_in_part, ("gc", "gr"))
    feat_grad = lax.dot_general(signal_grad, w_in, contract_last, preferred_element_type=F32)
    feat_grad = feat_grad.astype(jnp.bfloat16).reshape(rows, cols, width)
    return (feat_grad, w_in_grad, w_out_grad, row_grad, col_grad, b_grad, c_grad)


def solution(mesh):
    cell = P(("slide", "gr"), "gc", None)
    in_specs = (cell, cell, P(), P(), cell, cell, cell, cell, P(("slide", "gr"), "gc"))
    out_specs = (cell, P("slide", None), P("slide", None), cell, cell, cell, cell)
    return jax.shard_map(shards, mesh=mesh, in_specs=in_specs, out_specs=out_specs, check_vma=False)
```
